32 devices in a mesh: grp: 2 (over y), pts: 8 (over z, x), ctr: 2 (over core).
Axes of the slice: x: 2, y: 2, z: 4, core: 2. Of those that a mesh axis runs over, the one named last changes fastest.
Arguments:
- points: bfloat16 [3072, 128], P(('grp', 'pts')), parts along dimension 0, may hold values from -1.5 to 1.5
- curvature: bfloat16 [3072, 32], P(('grp', 'pts')), parts along dimension 0, may hold values from 0.019897461 to 0.25
- centers: bfloat16 [128, 131072], P(None, ('grp', 'pts', 'ctr')), parts along dimension 1, may hold values from -1.5 to 1.5
- coef: bfloat16 [32, 131072], P(None, ('grp', 'pts', 'ctr')), parts along dimension 1, may hold values from -1.1953125 to 1.1953125
Outputs:
- hvp: float32 [32, 131072], P(None, ('grp', 'pts', 'ctr')), parts along dimension 1
The draws below stay inside these ranges and needn't reach their ends.
There are 2 independent parts, one for each index of `grp`. The reference program is written for one: setup_inputs(seed, part) draws one part's arguments, and reference() takes and returns one part's arrays. A program takes and returns all parts, laid end to end along the dimension named above; each array names one. Nothing has to cross between parts.
All inputs are finite; a program needn't handle non-finite values.
Results may differ from the reference program's by a relative error of at most 0.0003.
Values may be sent and summed in bfloat16 or wider, within the bound.
A program may use at most 64 MiB of HBM per device.

```python
import math
import jax
import jax.numpy as jnp
from jax import lax

D = 128
LABELS = 32
CENTERS = 65536
POINTS = 1536


def block_levels(rng, extent, pieces, smallest, largest):
    gain = 1.0
    for position, blocks in pieces:
        heights = jax.random.uniform(jax.random.fold_in(jax.random.fold_in(rng, 6), position), (blocks,), jnp.float32, smallest / len(pieces), largest / len(pieces))
        gain = gain * jnp.repeat(jnp.exp(heights), extent[position] // blocks).reshape((-1,) + (1,) * (len(extent) - 1 - position))
    return gain


def bell_draw(own_key, dims, scale, limit, split=(), kind=jnp.bfloat16):
    result = scale * jax.random.normal(own_key, dims, jnp.float32)
    if split:
        result = result * block_levels(own_key, dims, split, -0.22, 0.18)
    return jnp.clip(result, -limit, limit).astype(kind)


def setup_inputs(seed: int = 0, part: int = 0) -> dict:
    streams_of = jax.random.split(jax.random.key(seed), 5)
    own_keys = jax.random.split(jax.random.fold_in(streams_of[4], part), 5)
    points = bell_draw(own_keys[0], (POINTS, D), 0.25, 1.5, ((0, 8),))
    curvature = jnp.clip(jnp.exp(math.log(0.25) - 2.5308688 * jax.random.uniform(own_keys[1], (POINTS, LABELS), jnp.float32) ** block_levels(own_keys[1], (POINTS, LABELS), ((0, 8),), -0.2, 0.2)), 0.019897461, 0.25).astype(jnp.bfloat16)
    centers = bell_draw(own_keys[2], (D, CENTERS), 0.25, 1.5, ((1, 16),))
    coef = bell_draw(own_keys[3], (LABELS, CENTERS), 0.2, 1.1953125, ((1, 16),))
    return dict(points=points, curvature=curvature, centers=centers, coef=coef)


def kernel_tile(points, sq_points, block, scale):
    sq_centers = jnp.sum(jnp.square(block.astype(jnp.float32)), axis=0)
    inner = jnp.dot(points, block, preferred_element_type=jnp.float32)
    dist = sq_points[:, None] + sq_centers[None, :] - 2.0 * inner
    return jnp.exp(-dist * scale).astype(jnp.bfloat16)


def reference(points, curvature, centers, coef):
    scale = 32.0 / D
    rows = points.shape[0]
    sq_points = jnp.sum(jnp.square(points.astype(jnp.float32)), axis=1)
    width = min(4096, CENTERS)
    count = CENTERS // width
    center_blocks = centers.reshape(D, count, width).transpose(1, 0, 2)
    coef_blocks = coef.reshape(LABELS, count, width).transpose(1, 0, 2)

    def accumulate(carry, pair):
        block, values = pair
        tile = kernel_tile(points, sq_points, block, scale)
        term = lax.dot_general(tile, values, (((1,), (1,)), ((), ())), preferred_element_type=jnp.float32)
        return carry + term, None

    tangent, unused = lax.scan(accumulate, jnp.zeros((rows, LABELS), jnp.float32), (center_blocks, coef_blocks))
    weighted = (curvature.astype(jnp.float32) * tangent).astype(jnp.bfloat16)

    def project(block):
        tile = kernel_tile(points, sq_points, block, scale)
        return lax.dot_general(weighted, tile, (((0,), (0,)), ((), ())), preferred_element_type=jnp.float32)

    parts = lax.map(project, center_blocks)
    return parts.transpose(1, 0, 2).reshape(LABELS, CENTERS)
```

```python
import functools
import math

import jax
import jax.numpy as jnp
from jax import lax
from jax.experimental import pallas as pl
from jax.experimental.pallas import tpu as pltpu
from jax.sharding import PartitionSpec as P

MESH = pl.DeviceIdType.MESH
F32, BF16 = jnp.float32, jnp.bfloat16
NT = (((1,), (1,)), ((), ()))


def xor(a, b, size):
    both, bit = 0, 1
    while bit < size:
        both = both + ((a // bit) % 2) * ((b // bit) % 2) * bit
        bit *= 2
    return a + b - 2 * both


def split3(x):
    high = x.astype(BF16).astype(F32)
    rest = x - high
    middle = rest.astype(BF16).astype(F32)
    low = (rest - middle).astype(BF16).astype(F32)
    return high, middle, low


def kernel(n, m, factor, points, curvature, centers, coef, out,
           near, tile, aug, part, got, weight, curve,
           p_send, p_recv, t_send, t_recv, w_send, w_recv):
    j, c = lax.axis_index("pts"), lax.axis_index("ctr")
    rows, depth = points.shape
    total = centers.shape[1]
    labels = coef.shape[0]
    count = n * m
    me = j * m + c
    wide = min(512, total)

    def place(t):
        other = xor(me, t, count)
        return {"pts": other // m, "ctr": other % m}

    barrier = pltpu.get_barrier_semaphore()

    def greet(t, carry):
        pl.semaphore_signal(barrier, inc=1, device_id=place(t), device_id_type=MESH)
        return carry

    lax.fori_loop(1, count, greet, 0)
    pl.semaphore_wait(barrier, count - 1)

    def point_copy(s):
        return pltpu.make_async_remote_copy(
            src_ref=points, dst_ref=near.at[j],
            send_sem=p_send.at[s], recv_sem=p_recv.at[s],
            device_id={"pts": xor(j, s, n)}, device_id_type=MESH,
        )

    def send_points(s, carry):
        point_copy(s).start()
        return carry

    lax.fori_loop(1, n, send_points, 0)

    def augment():
        block = centers[...].astype(F32)
        high, middle, low = split3(-0.5 * jnp.sum(block * block, axis=0, keepdims=True))
        spot = lax.broadcasted_iota(jnp.int32, (depth, total), 0)
        extra = jnp.where(spot < 6, 1.0, 0.0)
        for number, value in enumerate((high, middle, low)):
            extra = jnp.where(spot == number, value, extra)
        aug[0:depth, :] = centers[...]
        aug[depth : 2 * depth, :] = extra.astype(BF16)
        turned = curvature[...].astype(F32)
        for number in range(m):
            curve[number] = turned[number * (labels // m) : (number + 1) * (labels // m), :]

    augment()

    def pair(block, b):
        wider = block.astype(F32)
        high, middle, low = split3(-0.5 * jnp.sum(wider * wider, axis=1, keepdims=True))
        spot = lax.broadcasted_iota(jnp.int32, (rows, depth), 1)
        extra = jnp.where(spot < 3, 1.0, 0.0)
        for number, value in enumerate((high, middle, low)):
            extra = jnp.where(spot == number + 3, value, extra)
        left = jnp.concatenate([block, extra.astype(BF16)], axis=1)
        for start in range(0, total, wide):
            inner = jnp.dot(left, aug[:, start : start + wide], preferred_element_type=F32)
            tile[b, :, start : start + wide] = jnp.exp2(inner * factor).astype(BF16)
        value = lax.dot_general(coef[...], tile[b], NT, preferred_element_type=F32)
        for number in range(m):
            part[b, number] = value[number * (labels // m) : (number + 1) * (labels // m), :]

    def part_copy(s, d):
        t = s * m + d
        b, cc = xor(j, s, n), xor(c, d, m)
        return pltpu.make_async_remote_copy(
            src_ref=part.at[b, cc], dst_ref=got.at[t],
            send_sem=t_send.at[t], recv_sem=t_recv.at[t],
            device_id={"pts": b, "ctr": cc}, device_id_type=MESH,
        )

    pair(points[...], j)
    got[0] = part[j, c]
    for d in range(1, m):
        part_copy(0, d).start()

    def step(s, carry):
        b = xor(j, s, n)
        point_copy(s).wait_recv()
        pair(near[b], b)
        for d in range(m):
            part_copy(s, d).start()
        return carry

    lax.fori_loop(1, n, step, 0)

    def arrived(t, value):
        part_copy(t // m, t % m).wait_recv()
        return value + got[t]

    value = lax.fori_loop(1, count, arrived, got[0])
    weight[j, c] = (curve[c] * value).astype(BF16)

    def weight_copy(t):
        return pltpu.make_async_remote_copy(
            src_ref=weight.at[j, c], dst_ref=weight.at[j, c],
            send_sem=w_send.at[t], recv_sem=w_recv.at[t],
            device_id=place(t), device_id_type=MESH,
        )

    def send_weight(t, carry):
        weight_copy(t).start()
        return carry

    lax.fori_loop(1, count, send_weight, 0)

    def wait_weight(t, carry):
        weight_copy(t).wait_recv()
        return carry

    lax.fori_loop(1, count, wait_weight, 0)

    def project(i, carry):
        columns = pl.ds(pl.multiple_of(i * wide, wide), wide)

        def add(b, value):
            left = jnp.concatenate([weight[b, number] for number in range(m)], axis=0)
            return value + jnp.dot(left, tile[b, :, columns], preferred_element_type=F32)

        value = jnp.zeros((labels, wide), F32)
        if n <= 16:
            for b in range(n):
                value = add(b, value)
        else:
            value = lax.fori_loop(0, n, add, value)
        out[:, columns] = value
        return carry

    lax.fori_loop(0, total // wide, project, 0)

    def finish(t, carry):
        part_copy(t // m, t % m).wait_send()
        weight_copy(t).wait_send()
        return carry

    lax.fori_loop(1, count, finish, 0)

    def finish_points(s, carry):
        point_copy(s).wait_send()
        return carry

    lax.fori_loop(1, n, finish_points, 0)


def solution(mesh):
    n, m = mesh.shape["pts"], mesh.shape["ctr"]

    def on_device(points, curvature, centers, coef):
        rows, depth = points.shape
        labels, total = coef.shape
        factor = 2.0 * (32.0 / depth) * math.log2(math.e)
        share = labels // m
        return pl.pallas_call(
            functools.partial(kernel, n, m, factor),
            out_shape=jax.ShapeDtypeStruct((labels, total), F32),
            in_specs=[pl.BlockSpec(memory_space=pltpu.VMEM)] * 4,
            out_specs=pl.BlockSpec(memory_space=pltpu.VMEM),
            scratch_shapes=[
                pltpu.VMEM((n, rows, depth), BF16),
                pltpu.VMEM((n, rows, total), BF16),
                pltpu.VMEM((2 * depth, total), BF16),
                pltpu.VMEM((n, m, share, rows), F32),
                pltpu.VMEM((n * m, share, rows), F32),
                pltpu.VMEM((n, m, share, rows), BF16),
                pltpu.VMEM((m, share, rows), F32),
                pltpu.SemaphoreType.DMA((n,)),
                pltpu.SemaphoreType.DMA((n,)),
                pltpu.SemaphoreType.DMA((n * m,)),
                pltpu.SemaphoreType.DMA((n * m,)),
                pltpu.SemaphoreType.DMA((n * m,)),
                pltpu.SemaphoreType.DMA((n * m,)),
            ],
            compiler_params=pltpu.CompilerParams(
                collective_id=0, has_side_effects=True, vmem_limit_bytes=56 << 20
            ),
        )(points, curvature.T, centers, coef)

    in_specs = (
        P(("grp", "pts"), None),
        P(("grp", "pts"), None),
        P(None, ("grp", "pts", "ctr")),
        P(None, ("grp", "pts", "ctr")),
    )
    out_specs = P(None, ("grp", "pts", "ctr"))
    return jax.shard_map(
        on_device, mesh=mesh, in_specs=in_specs, out_specs=out_specs, check_vma=False
    )
```

```python
import functools
import math

import jax
import jax.numpy as jnp
from jax import lax
from jax.experimental import pallas as pl
from jax.experimental.pallas import tpu as pltpu
from jax.sharding import PartitionSpec as P

MESH = pl.DeviceIdType.MESH
F32, BF16 = jnp.float32, jnp.bfloat16


def xor(a, b, size):
    both, bit = 0, 1
    while bit < size:
        both = both + ((a // bit) % 2) * ((b // bit) % 2) * bit
        bit *= 2
    return a + b - 2 * both


def split3(x):
    high = x.astype(BF16).astype(F32)
    rest = x - high
    middle = rest.astype(BF16).astype(F32)
    low = (rest - middle).astype(BF16).astype(F32)
    return high, middle, low


def kernel(n, factor, points_in, curvature_in, centers_in, coef_in, out,
           points, curvature, centers, coef, near, tile, aug, centers2, coef2, turned, part, got, weight, mine, ours, theirs,
           p_send, p_recv, t_send, t_recv, w_send, w_recv, c_send, c_recv, o_send, o_recv, l_in, l_out):
    j, c = lax.axis_index("pts"), lax.axis_index("ctr")
    half, depth = points.shape[0] // 2, points.shape[1]
    labels, total = coef.shape
    wide = mine.shape[2]
    chunks = total // wide
    pairs = n // 2
    sibling = {"ctr": 1 - c}

    def peer(s):
        return {"pts": xor(j, s, n)}

    barrier = pltpu.get_barrier_semaphore()
    pl.semaphore_signal(barrier, inc=1, device_id=sibling, device_id_type=MESH)

    def greet(s, carry):
        pl.semaphore_signal(barrier, inc=1, device_id=peer(s), device_id_type=MESH)
        return carry

    lax.fori_loop(1, n, greet, 0)

    loads = [
        pltpu.make_async_copy(source, target, l_in.at[number])
        for number, (source, target) in enumerate(
            ((points_in, points), (centers_in, centers), (coef_in, coef), (curvature_in, curvature))
        )
    ]
    for load in loads:
        load.start()

    def augment(side, source, values):
        turned[side] = values[...].astype(F32).T.astype(BF16)
        block = source[...].astype(F32)
        high, middle, low = split3(-0.5 * jnp.sum(block * block, axis=0, keepdims=True))
        spot = lax.broadcasted_iota(jnp.int32, (depth, total), 0)
        extra = jnp.where(spot < 6, 1.0, 0.0)
        for number, value in enumerate((high, middle, low)):
            extra = jnp.where(spot == number, value, extra)
        aug[side, 0:depth, :] = source[...]
        aug[side, depth : 2 * depth, :] = extra.astype(BF16)

    own = pl.ds(pl.multiple_of(c * half, half), half)
    for load in loads:
        load.wait()
    near[0:half, :] = points[own, :]
    pl.semaphore_wait(barrier, n)

    def copy(source, target, send, receive, device):
        return pltpu.make_async_remote_copy(
            src_ref=source, dst_ref=target, send_sem=send, recv_sem=receive,
            device_id=device, device_id_type=MESH,
        )

    def point_copy(s):
        slot = pl.ds(pl.multiple_of(s * half, half), half)
        return copy(near.at[pl.ds(0, half)], near.at[slot], p_send.at[s], p_recv.at[s], peer(s))

    def each(first, last, act):
        def body(s, carry):
            act(s)
            return carry

        lax.fori_loop(first, last, body, 0)

    center_copy = copy(centers, centers2, c_send.at[0], c_recv.at[0], sibling)
    coef_copy = copy(coef, coef2, c_send.at[1], c_recv.at[1], sibling)
    point_copy(1).start()
    center_copy.start()
    coef_copy.start()

    def turn(i):
        later = i + pairs // 2 - 1
        return later - (later // pairs) * (pairs - 1)

    def send_points(i):
        point_copy(2 * turn(i)).start()
        point_copy(2 * turn(i) + 1).start()

    each(1, pairs, send_points)
    augment(0, centers, coef)

    def part_copy(s):
        return copy(part.at[s], got.at[s], t_send.at[s], t_recv.at[s], peer(s))

    def left_side(i):
        block = near[pl.ds(pl.multiple_of(i * 2 * half, 2 * half), 2 * half), :]
        wider = block.astype(F32)
        high, middle, low = split3(-0.5 * jnp.sum(wider * wider, axis=1, keepdims=True))
        spot = lax.broadcasted_iota(jnp.int32, (2 * half, depth), 1)
        extra = jnp.where(spot < 3, 1.0, 0.0)
        for number, value in enumerate((high, middle, low)):
            extra = jnp.where(spot == number + 3, value, extra)
        return jnp.concatenate([block, extra.astype(BF16)], axis=1)

    def pair(i, left, side):
        for start in range(0, total, wide):
            inner = jnp.dot(
                left, aug[side, :, start : start + wide], preferred_element_type=F32
            )
            tile[i, side, :, start : start + wide] = jnp.exp2(inner * factor).astype(BF16)
        return jnp.dot(tile[i, side], turned[side], preferred_element_type=F32)

    def keep(i, value):
        value = value.T
        part[2 * i] = value[:, 0:half]
        part[2 * i + 1] = value[:, half : 2 * half]

    point_copy(1).wait_recv()
    left = left_side(0)
    value = pair(0, left, 0)
    center_copy.wait_recv()
    coef_copy.wait_recv()
    augment(1, centers2, coef2)
    keep(0, value + pair(0, left, 1))
    part_copy(1).start()
    got[0] = part[0]

    def step(number):
        i = turn(number)
        point_copy(2 * i).wait_recv()
        point_copy(2 * i + 1).wait_recv()
        left = left_side(i)
        keep(i, pair(i, left, 0) + pair(i, left, 1))
        part_copy(2 * i).start()
        part_copy(2 * i + 1).start()

    each(1, pairs, step)

    def arrived(s, value):
        part_copy(s).wait_recv()
        return value + got[s]

    value = lax.fori_loop(1, n, arrived, got[0])
    saved = jnp.where(c == 0, curvature[:, 0:half].astype(F32), curvature[:, half : 2 * half].astype(F32))
    weight[0] = (saved * value).astype(BF16)

    def weight_copy(s):
        return copy(weight.at[0], weight.at[s], w_send.at[s], w_recv.at[s], peer(s))

    each(1, n, lambda s: weight_copy(n - s).start())

    def columns(number):
        return pl.ds(pl.multiple_of(number * wide, wide), wide)

    def join(i):
        return jnp.concatenate([weight[2 * i], weight[2 * i + 1]], axis=1)

    def project(left, i, side, number):
        return jnp.dot(left, tile[i, side, :, columns(number)], preferred_element_type=F32)

    def share_copy(number):
        return copy(mine.at[number], theirs.at[number], o_send.at[number], o_recv.at[number], sibling)

    def out_copy(number):
        return pltpu.make_async_copy(ours.at[number], out.at[:, columns(number)], l_out.at[number])

    weight_copy(1).wait_recv()
    left = join(0)

    def begin(number):
        mine[number] = project(left, 0, 1, number)
        ours[number] = project(left, 0, 0, number)

    each(0, chunks, begin)

    def middle(i):
        weight_copy(2 * i).wait_recv()
        weight_copy(2 * i + 1).wait_recv()
        left = join(i)

        def more(number):
            mine[number] += project(left, i, 1, number)
            ours[number] += project(left, i, 0, number)

        each(0, chunks, more)

    each(1, pairs - 1, middle)
    last = pairs - 1
    weight_copy(2 * last).wait_recv()
    weight_copy(2 * last + 1).wait_recv()
    left_last = join(last)

    def give(number):
        mine[number] += project(left_last, last, 1, number)
        share_copy(number).start()

    def take(number):
        value = ours[number] + project(left_last, last, 0, number)
        share_copy(number).wait_recv()
        ours[number] = value + theirs[number]
        out_copy(number).start()

    each(0, chunks, give)
    each(0, chunks, take)

    def finish(s):
        point_copy(s).wait_send()
        part_copy(s).wait_send()
        weight_copy(s).wait_send()

    each(1, n, finish)
    center_copy.wait_send()
    coef_copy.wait_send()
    each(0, chunks, lambda number: share_copy(number).wait_send())
    each(0, chunks, lambda number: out_copy(number).wait())


def solution(mesh):
    n = mesh.shape["pts"]

    def on_device(points, curvature, centers, coef):
        rows, depth = points.shape
        labels, total = coef.shape
        factor = 2.0 * (32.0 / depth) * math.log2(math.e)
        half = rows // 2
        wide = min(512, total)
        dma = pltpu.SemaphoreType.DMA
        return pl.pallas_call(
            functools.partial(kernel, n, factor),
            out_shape=jax.ShapeDtypeStruct((labels, total), F32),
            in_specs=[pl.BlockSpec(memory_space=pltpu.HBM)] * 4,
            out_specs=pl.BlockSpec(memory_space=pltpu.HBM),
            scratch_shapes=[
                pltpu.VMEM((rows, depth), BF16),
                pltpu.VMEM((labels, rows), BF16),
                pltpu.VMEM((depth, total), BF16),
                pltpu.VMEM((labels, total), BF16),
                pltpu.VMEM((n * half, depth), BF16),
                pltpu.VMEM((n // 2, 2, rows, total), BF16),
                pltpu.VMEM((2, 2 * depth, total), BF16),
                pltpu.VMEM((depth, total), BF16),
                pltpu.VMEM((labels, total), BF16),
                pltpu.VMEM((2, total, labels), BF16),
                pltpu.VMEM((n, labels, half), F32),
                pltpu.VMEM((n, labels, half), F32),
                pltpu.VMEM((n, labels, half), BF16),
                pltpu.VMEM((total // wide, labels, wide), F32),
                pltpu.VMEM((total // wide, labels, wide), F32),
                pltpu.VMEM((total // wide, labels, wide), F32),
                dma((n,)), dma((n,)), dma((n,)), dma((n,)), dma((n,)), dma((n,)),
                dma((2,)), dma((2,)), dma((total // wide,)), dma((total // wide,)),
                dma((4,)), dma((total // wide,)),
            ],
            compiler_params=pltpu.CompilerParams(
                collective_id=0, has_side_effects=True, vmem_limit_bytes=56 << 20
            ),
        )(points, curvature.T, centers, coef)

    in_specs = (
        P(("grp", "pts"), None),
        P(("grp", "pts"), None),
        P(None, ("grp", "pts", "ctr")),
        P(None, ("grp", "pts", "ctr")),
    )
    out_specs = P(None, ("grp", "pts", "ctr"))
    return jax.shard_map(
        on_device, mesh=mesh, in_specs=in_specs, out_specs=out_specs, check_vma=False
    )
```

```python
import functools
import math

import jax
import jax.numpy as jnp
from jax import lax
from jax.experimental import pallas as pl
from jax.experimental.pallas import tpu as pltpu
from jax.sharding import PartitionSpec as P

MESH = pl.DeviceIdType.MESH
F32, BF16 = jnp.float32, jnp.bfloat16


def xor(a, b, size):
    both, bit = 0, 1
    while bit < size:
        both = both + ((a // bit) % 2) * ((b // bit) % 2) * bit
        bit *= 2
    return a + b - 2 * both


def split3(x):
    high = x.astype(BF16).astype(F32)
    rest = x - high
    middle = rest.astype(BF16).astype(F32)
    low = (rest - middle).astype(BF16).astype(F32)
    return high, middle, low


def kernel(n, factor, points_in, curvature_in, centers_in, coef_in, out,
           points, curvature, centers, coef, near, tile, aug, centers2, coef2, turned, part, got, weight, mine, ours, theirs,
           p_send, p_recv, t_send, t_recv, w_send, w_recv, c_send, c_recv, o_send, o_recv, l_in, l_out):
    j, c = lax.axis_index("pts"), lax.axis_index("ctr")
    half, depth = points.shape[0] // 2, points.shape[1]
    labels, total = coef.shape
    wide = mine.shape[2]
    chunks = total // wide
    pairs = n // 2
    broad = min(1024, total)
    sibling = {"ctr": 1 - c}

    def peer(s):
        return {"pts": xor(j, s, n)}

    barrier = pltpu.get_barrier_semaphore()
    pl.semaphore_signal(barrier, inc=1, device_id=sibling, device_id_type=MESH)

    def greet(s, carry):
        pl.semaphore_signal(barrier, inc=1, device_id=peer(s), device_id_type=MESH)
        return carry

    lax.fori_loop(1, n, greet, 0)

    loads = [
        pltpu.make_async_copy(source, target, l_in.at[number])
        for number, (source, target) in enumerate(
            ((points_in, points), (centers_in, centers), (coef_in, coef), (curvature_in, curvature))
        )
    ]
    for load in loads:
        load.start()

    def augment(side, source, values):
        turned[side] = values[...].astype(F32).T.astype(BF16)
        block = source[...].astype(F32)
        high, middle, low = split3(-0.5 * jnp.sum(block * block, axis=0, keepdims=True))
        spot = lax.broadcasted_iota(jnp.int32, (depth, total), 0)
        extra = jnp.where(spot < 6, 1.0, 0.0)
        for number, value in enumerate((high, middle, low)):
            extra = jnp.where(spot == number, value, extra)
        aug[side, 0:depth, :] = source[...]
        aug[side, depth : 2 * depth, :] = extra.astype(BF16)

    own = pl.ds(pl.multiple_of(c * half, half), half)
    for load in loads:
        load.wait()
    near[0:half, :] = points[own, :]
    pl.semaphore_wait(barrier, n)

    def copy(source, target, send, receive, device):
        return pltpu.make_async_remote_copy(
            src_ref=source, dst_ref=target, send_sem=send, recv_sem=receive,
            device_id=device, device_id_type=MESH,
        )

    def point_copy(s):
        slot = pl.ds(pl.multiple_of(s * half, half), half)
        return copy(near.at[pl.ds(0, half)], near.at[slot], p_send.at[s], p_recv.at[s], peer(s))

    def each(first, last, act):
        def body(s, carry):
            act(s)
            return carry

        lax.fori_loop(first, last, body, 0)

    center_copy = copy(centers, centers2, c_send.at[0], c_recv.at[0], sibling)
    coef_copy = copy(coef, coef2, c_send.at[1], c_recv.at[1], sibling)
    point_copy(1).start()
    center_copy.start()
    coef_copy.start()

    def turn(i):
        later = i + pairs // 2 - 1
        return later - (later // pairs) * (pairs - 1)

    def send_points(i):
        point_copy(2 * turn(i)).start()
        point_copy(2 * turn(i) + 1).start()

    each(1, pairs, send_points)
    augment(0, centers, coef)

    def part_copy(s):
        return copy(part.at[s], got.at[s], t_send.at[s], t_recv.at[s], peer(s))

    def left_side(i):
        block = near[pl.ds(pl.multiple_of(i * 2 * half, 2 * half), 2 * half), :]
        wider = block.astype(F32)
        high, middle, low = split3(-0.5 * jnp.sum(wider * wider, axis=1, keepdims=True))
        spot = lax.broadcasted_iota(jnp.int32, (2 * half, depth), 1)
        extra = jnp.where(spot < 3, 1.0, 0.0)
        for number, value in enumerate((high, middle, low)):
            extra = jnp.where(spot == number + 3, value, extra)
        return jnp.concatenate([block, extra.astype(BF16)], axis=1)

    def pair(i, left, side):
        for start in range(0, total, broad):
            inner = jnp.dot(
                left, aug[side, :, start : start + broad], preferred_element_type=F32
            )
            tile[i, side, :, start : start + broad] = jnp.exp2(inner * factor).astype(BF16)
        return jnp.dot(tile[i, side], turned[side], preferred_element_type=F32)

    def keep(i, value):
        value = value.T
        part[2 * i] = value[:, 0:half]
        part[2 * i + 1] = value[:, half : 2 * half]

    point_copy(1).wait_recv()
    left = left_side(0)
    value = pair(0, left, 0)
    center_copy.wait_recv()
    coef_copy.wait_recv()
    augment(1, centers2, coef2)
    keep(0, value + pair(0, left, 1))
    part_copy(1).start()
    got[0] = part[0]

    def step(number):
        i = turn(number)
        point_copy(2 * i).wait_recv()
        point_copy(2 * i + 1).wait_recv()
        left = left_side(i)
        keep(i, pair(i, left, 0) + pair(i, left, 1))
        part_copy(2 * i).start()
        part_copy(2 * i + 1).start()

    each(1, pairs, step)

    def arrived(s, value):
        part_copy(s).wait_recv()
        return value + got[s]

    value = lax.fori_loop(1, n, arrived, got[0])
    saved = jnp.where(c == 0, curvature[:, 0:half].astype(F32), curvature[:, half : 2 * half].astype(F32))
    weight[0] = (saved * value).astype(BF16)

    def weight_copy(s):
        return copy(weight.at[0], weight.at[s], w_send.at[s], w_recv.at[s], peer(s))

    each(1, n, lambda s: weight_copy(n - s).start())

    def columns(number):
        return pl.ds(pl.multiple_of(number * wide, wide), wide)

    def join(i):
        return jnp.concatenate([weight[2 * i], weight[2 * i + 1]], axis=1)

    def project(left, i, side, number):
        return jnp.dot(left, tile[i, side, :, columns(number)], preferred_element_type=F32)

    def share_copy(number):
        return copy(mine.at[number], theirs.at[number], o_send.at[number], o_recv.at[number], sibling)

    def out_copy(number):
        return pltpu.make_async_copy(ours.at[number], out.at[:, columns(number)], l_out.at[number])

    weight_copy(1).wait_recv()
    left = join(0)

    def begin(number):
        mine[number] = project(left, 0, 1, number)
        ours[number] = project(left, 0, 0, number)

    each(0, chunks, begin)

    def middle(i):
        weight_copy(2 * i).wait_recv()
        weight_copy(2 * i + 1).wait_recv()
        left = join(i)

        def more(number):
            mine[number] += project(left, i, 1, number)
            ours[number] += project(left, i, 0, number)

        each(0, chunks, more)

    each(1, pairs - 1, middle)
    last = pairs - 1
    weight_copy(2 * last).wait_recv()
    weight_copy(2 * last + 1).wait_recv()
    left_last = join(last)

    def give(number):
        mine[number] += project(left_last, last, 1, number)
        share_copy(number).start()

    def take(number):
        value = ours[number] + project(left_last, last, 0, number)
        share_copy(number).wait_recv()
        ours[number] = value + theirs[number]
        out_copy(number).start()

    each(0, chunks, give)
    each(0, chunks, take)

    def finish(s):
        point_copy(s).wait_send()
        part_copy(s).wait_send()
        weight_copy(s).wait_send()

    each(1, n, finish)
    center_copy.wait_send()
    coef_copy.wait_send()
    each(0, chunks, lambda number: share_copy(number).wait_send())
    each(0, chunks, lambda number: out_copy(number).wait())


def solution(mesh):
    n = mesh.shape["pts"]

    def on_device(points, curvature, centers, coef):
        rows, depth = points.shape
        labels, total = coef.shape
        factor = 2.0 * (32.0 / depth) * math.log2(math.e)
        half = rows // 2
        wide = min(2048, total)
        dma = pltpu.SemaphoreType.DMA
        return pl.pallas_call(
            functools.partial(kernel, n, factor),
            out_shape=jax.ShapeDtypeStruct((labels, total), F32),
            in_specs=[pl.BlockSpec(memory_space=pltpu.HBM)] * 4,
            out_specs=pl.BlockSpec(memory_space=pltpu.HBM),
            scratch_shapes=[
                pltpu.VMEM((rows, depth), BF16),
                pltpu.VMEM((labels, rows), BF16),
                pltpu.VMEM((depth, total), BF16),
                pltpu.VMEM((labels, total), BF16),
                pltpu.VMEM((n * half, depth), BF16),
                pltpu.VMEM((n // 2, 2, rows, total), BF16),
                pltpu.VMEM((2, 2 * depth, total), BF16),
                pltpu.VMEM((depth, total), BF16),
                pltpu.VMEM((labels, total), BF16),
                pltpu.VMEM((2, total, labels), BF16),
                pltpu.VMEM((n, labels, half), F32),
                pltpu.VMEM((n, labels, half), F32),
                pltpu.VMEM((n, labels, half), BF16),
                pltpu.VMEM((total // wide, labels, wide), F32),
                pltpu.VMEM((total // wide, labels, wide), F32),
                pltpu.VMEM((total // wide, labels, wide), F32),
                dma((n,)), dma((n,)), dma((n,)), dma((n,)), dma((n,)), dma((n,)),
                dma((2,)), dma((2,)), dma((total // wide,)), dma((total // wide,)),
                dma((4,)), dma((total // wide,)),
            ],
            compiler_params=pltpu.CompilerParams(
                collective_id=0, has_side_effects=True, vmem_limit_bytes=56 << 20
            ),
        )(points, curvature.T, centers, coef)

    in_specs = (
        P(("grp", "pts"), None),
        P(("grp", "pts"), None),
        P(None, ("grp", "pts", "ctr")),
        P(None, ("grp", "pts", "ctr")),
    )
    out_specs = P(None, ("grp", "pts", "ctr"))
    return jax.shard_map(
        on_device, mesh=mesh, in_specs=in_specs, out_specs=out_specs, check_vma=False
    )
```
